32 devices in a mesh: band: 8 (over z, x), domain: 4 (over y, core).
Axes of the slice: x: 2, y: 2, z: 4, core: 2. Of those that a mesh axis runs over, the one named last changes fastest.
Arguments:
- orbitals: float32 [256, 4096], P('band', 'domain'), may hold values from -12 to 12
- potential: float32 [4096], P('domain'), may hold values from -9 to 4.5
- stencil: int32 [36, 4096], P(None, 'domain'), may hold values from 0 to 1536, as said below
- send_list: int32 [2, 1024], P(None, 'domain'), may hold values from 0 to 1023, as said below
- send_count: int32 [2, 4], P(None, 'domain'), may hold values from 0 to 256, as said below
Outputs:
- filtered: float32 [256, 4096], P('band', 'domain')
- correlation: float32 [256, 256], P('band', 'domain')
- subspace: float32 [256, 256], P('band', 'domain')
The draws below stay inside these ranges and needn't reach their ends.
Inputs may be any that keep to these rules, and one draw needn't show every extreme that they name: `stencil`: entries below 1024 name a slot of the point's own subdomain; entries from 1024 on name only live boundary rows of an existing neighbouring subdomain; 1536 marks a neighbour outside the cluster. `send_list`: each list of 256 entries holds distinct slots of the sending subdomain. `send_count`: row 0 counts the rows subdomain d sends to d + 1, row 1 those it sends to d - 1; zero toward a missing neighbour; 256 is reached in every draw.
All inputs are finite; a program needn't handle non-finite values.
Results may differ from the reference program's by a relative error of at most 0.00015.
Values sent between devices are 32-bit elements; how exact they have to be, the bound alone decides.
A program may use at most 128 MiB of HBM per device.

```python
import jax
import jax.numpy as jnp
from jax import lax

ORBS = 256
PTS = 1024
NB = 36
DEGREE = 4
CAP = 256
NPTS = 4096
N_DOMAIN = 4


def count_table(key):
    domains = NPTS // PTS
    inner_key = jax.random.fold_in(key, 101)
    first_key, second_key = jax.random.split(inner_key)
    face_index = jnp.arange(domains, dtype=jnp.int32)
    offset = 2 * face_index + 2 - domains
    weight = domains * domains - offset * offset
    middle = domains // 2 - 1
    upward = weight * jax.random.randint(first_key, (domains,), CAP // 2, CAP + 1) // (domains * domains)
    downward = weight * jax.random.randint(second_key, (domains,), CAP // 2, CAP + 1) // (domains * domains)
    upward = jnp.where(face_index == middle, CAP, upward)
    downward = jnp.where(face_index == middle, CAP, downward)
    upward = jnp.where(face_index < domains - 1, upward, 0)
    down_shifted = jnp.concatenate([jnp.zeros((1,), jnp.int32), downward[:-1].astype(jnp.int32)])
    return jnp.stack([upward.astype(jnp.int32), down_shifted]).astype(jnp.int32)


def draw_send_count(key, part):
    return count_table(key)


def draw_stencil(key, part):
    counts = count_table(key)
    below = jnp.concatenate([jnp.zeros((1,), jnp.int32), counts[0, :-1]])
    above = jnp.concatenate([counts[1, 1:], jnp.zeros((1,), jnp.int32)])
    owner_index = jnp.arange(NPTS, dtype=jnp.int32) // PTS
    below_point = below[owner_index][None, :]
    above_point = above[owner_index][None, :]
    inner_key = jax.random.fold_in(key, 202)
    kind_key, local_key, low_key, high_key = jax.random.split(inner_key, 4)
    category = jax.random.randint(kind_key, (NB, NPTS), 0, 100)
    local_slot = jax.random.randint(local_key, (NB, NPTS), 0, PTS)
    low_slot = jax.random.randint(low_key, (NB, NPTS), 0, jnp.maximum(below_point, 1))
    high_slot = jax.random.randint(high_key, (NB, NPTS), 0, jnp.maximum(above_point, 1))
    result = local_slot
    result = jnp.where((category >= 76) & (category < 88) & (below_point > 0), PTS + low_slot, result)
    result = jnp.where((category >= 88) & (category < 98) & (above_point > 0), PTS + CAP + high_slot, result)
    result = jnp.where(category >= 98, PTS + 2 * CAP, result)
    return result.astype(jnp.int32)


def draw_send_list(key, part):
    domains = NPTS // PTS
    list_keys = jax.random.split(jax.random.fold_in(key, 303), 2 * domains)
    chosen = jax.vmap(lambda subkey: jax.random.permutation(subkey, PTS)[:CAP])(list_keys)
    return chosen.reshape(2, domains * CAP).astype(jnp.int32)


def draw_potential(key, part):
    domains = NPTS // PTS
    owner_index = (jnp.arange(NPTS) // PTS).astype(jnp.float32)
    rising = owner_index / max(domains - 1, 1)
    uniform_part = jax.random.uniform(jax.random.fold_in(key, 404), (NPTS,), jnp.float32, -1.0, 0.5)
    domain_scale = 1.0 + 2.0 * rising
    return (domain_scale * uniform_part).astype(jnp.float32)


def draw_orbitals(key, part):
    noise_key, sign_key, level_key = jax.random.split(jax.random.fold_in(key, 505), 3)
    noise_part = jax.random.truncated_normal(noise_key, -4.0, 4.0, (ORBS, NPTS), jnp.float32)
    level = jax.random.uniform(level_key, (ORBS, 1), jnp.float32, 3.0, 5.0)
    sign_pick = jax.random.randint(sign_key, (ORBS, 1), 0, 2)
    signed_level = jnp.where(sign_pick == 0, -level, level)
    return (noise_part + signed_level).astype(jnp.float32)


def setup_inputs(seed: int = 0) -> dict:
    key_list = jax.random.split(jax.random.key(seed), 6)
    return {
        "orbitals": draw_orbitals(jax.random.fold_in(key_list[5], 71), 0),
        "potential": draw_potential(jax.random.fold_in(key_list[5], 71), 0),
        "stencil": draw_stencil(jax.random.fold_in(key_list[5], 71), 0),
        "send_list": draw_send_list(jax.random.fold_in(key_list[5], 71), 0),
        "send_count": draw_send_count(jax.random.fold_in(key_list[5], 71), 0),
    }


WEIGHTS = (-5369.0 / 1800.0, 12.0 / 7.0, -15.0 / 56.0, 10.0 / 189.0, -1.0 / 112.0, 2.0 / 1925.0, -1.0 / 16632.0)
KINETIC = 50.0 / 9.0
CUT_SHARE = 0.1
SPECTRAL_REACH = KINETIC * 3.0 * (abs(WEIGHTS[0]) + 2.0 * (abs(WEIGHTS[1]) + abs(WEIGHTS[2]) + abs(WEIGHTS[3]) + abs(WEIGHTS[4]) + abs(WEIGHTS[5]) + abs(WEIGHTS[6])))


def apply_operator(values, potential, stencil, send_list, send_count):
    orb_total = values.shape[0]
    blocks = values.reshape(orb_total, N_DOMAIN, PTS)
    list_blocks = send_list.reshape(2, N_DOMAIN, CAP)
    live_slots = lax.broadcasted_iota(jnp.int32, (2, N_DOMAIN, CAP), 2) < send_count[:, :, None]
    sent_rows = jax.vmap(lambda block_values, chosen_slots: block_values[:, chosen_slots], in_axes=(1, 1), out_axes=1)(blocks, list_blocks)
    sent_rows = jnp.where(jnp.transpose(live_slots, (1, 0, 2))[None], sent_rows, jnp.zeros_like(sent_rows))
    up_rows = sent_rows[:, :, 0]
    down_rows = sent_rows[:, :, 1]
    empty_rows = jnp.zeros((orb_total, 1, CAP), values.dtype)
    from_below = jnp.concatenate([empty_rows, up_rows[:, :-1]], axis=1)
    from_above = jnp.concatenate([down_rows[:, 1:], empty_rows], axis=1)
    zero_column = jnp.zeros((orb_total, N_DOMAIN, 1), values.dtype)
    buffer = jnp.concatenate([blocks, from_below, from_above, zero_column], axis=2)
    stencil_blocks = stencil.reshape(NB, N_DOMAIN, PTS)

    def one_domain(inputs):
        domain_buffer, neighbours, potential_block, own_values = inputs
        near_sum = jnp.zeros_like(own_values)
        for distance in range(6):
            cycle_sum = jnp.zeros_like(own_values)
            for member in range(6):
                cycle_sum = cycle_sum + domain_buffer[:, neighbours[6 * distance + member]]
            near_sum = near_sum + WEIGHTS[distance + 1] * cycle_sum
        return potential_block * own_values - KINETIC * (3.0 * WEIGHTS[0] * own_values + near_sum)

    result = lax.map(one_domain, (jnp.transpose(buffer, (1, 0, 2)), jnp.transpose(stencil_blocks, (1, 0, 2)), potential.reshape(N_DOMAIN, PTS), jnp.transpose(blocks, (1, 0, 2))))
    return jnp.transpose(result, (1, 0, 2)).reshape(orb_total, NPTS)


def filter_block(orbitals, operator_fn, lowest, highest):
    top_bound = highest + SPECTRAL_REACH
    cut_point = lowest + CUT_SHARE * (top_bound - lowest)
    half_width = (top_bound - cut_point) / 2.0
    centre = (top_bound + cut_point) / 2.0
    sigma_now = half_width / (lowest - centre)
    sigma_scale = 2.0 / sigma_now
    previous = orbitals
    current = (sigma_now / half_width) * (operator_fn(orbitals) - centre * orbitals)
    for order_index in range(2, DEGREE + 1):
        sigma_next = 1.0 / (sigma_scale - sigma_now)
        following = (2.0 * sigma_next / half_width) * (operator_fn(current) - centre * current) - (sigma_now * sigma_next) * previous
        previous = current
        current = following
        sigma_now = sigma_next
    return current


def reference(orbitals, potential, stencil, send_list, send_count):
    lowest = jnp.min(potential)
    highest = jnp.max(potential)

    def operator_fn(values):
        return apply_operator(values, potential, stencil, send_list, send_count)

    filtered = filter_block(orbitals, operator_fn, lowest, highest)
    applied = operator_fn(filtered)
    correlation = jnp.dot(filtered, filtered.T, preferred_element_type=jnp.float32, precision=lax.Precision.HIGHEST) / NPTS
    subspace = jnp.dot(filtered, applied.T, preferred_element_type=jnp.float32, precision=lax.Precision.HIGHEST) / NPTS
    return filtered, correlation, subspace
```

```python
import functools

import jax
import jax.numpy as jnp
from jax import lax
from jax.experimental import pallas as pl
from jax.experimental.pallas import tpu as pltpu
from jax.sharding import PartitionSpec as P

DEGREE = 4
WEIGHTS = (
    -5369.0 / 1800.0,
    12.0 / 7.0,
    -15.0 / 56.0,
    10.0 / 189.0,
    -1.0 / 112.0,
    2.0 / 1925.0,
    -1.0 / 16632.0,
)
KINETIC = 50.0 / 9.0
CUT_SHARE = 0.1
SPECTRAL_REACH = KINETIC * 3.0 * (abs(WEIGHTS[0]) + 2.0 * sum(abs(w) for w in WEIGHTS[1:]))
MESH = pl.DeviceIdType.MESH
DIGITS = 8
f32, bf16, i32 = jnp.float32, jnp.bfloat16, jnp.int32


def remote(src, dst, send_sem, recv_sem, device_id):
    return pltpu.make_async_remote_copy(
        src_ref=src,
        dst_ref=dst,
        send_sem=send_sem,
        recv_sem=recv_sem,
        device_id=device_id,
        device_id_type=MESH,
    )


def split(x):
    hi = x.astype(bf16)
    lo = (x - hi.astype(f32)).astype(bf16)
    return hi, lo


def dot3(stacked, hi_rows, right_hi, right_lo):
    both = jnp.dot(stacked, right_hi, preferred_element_type=f32)
    low = jnp.dot(stacked[:hi_rows], right_lo, preferred_element_type=f32)
    return both[:hi_rows] + both[hi_rows:] + low


def kernel(D, B, gram, orb_ref, pot_ref, sten_ref, list_ref, count_ref, filt_ref, out_ref, *scratch):
    ah, al, sel, slot, unit, mm, sent, halo, mm_ss, mm_rs, h_ss, h_rs = scratch[:12]
    d = lax.axis_index("domain")
    b = lax.axis_index("band")
    R, N = orb_ref.shape
    cap = list_ref.shape[1]
    groups = (N + 2 * cap) // DIGITS

    halo[...] = jnp.zeros_like(halo)
    barrier = pltpu.get_barrier_semaphore()
    for o in range(1, D):
        pl.semaphore_signal(
            barrier, inc=1, device_id={"domain": lax.rem(d + o, D)}, device_id_type=MESH
        )
    if gram:
        for o in range(1, B):
            pl.semaphore_signal(
                barrier, inc=1, device_id={"band": lax.rem(b + o, B)}, device_id_type=MESH
            )

    pot = pot_ref[...]
    mm[0, 0:1] = jnp.broadcast_to(jnp.min(pot, axis=1, keepdims=True), (1, 128))
    mm[0, 1:2] = jnp.broadcast_to(jnp.max(pot, axis=1, keepdims=True), (1, 128))
    live = lax.broadcasted_iota(i32, (2, cap), 1) < count_ref[...]
    lists = jnp.where(live, list_ref[...], -1)

    def sel_body(step, carry):
        start = pl.multiple_of(step * 128, 128)
        rows = lax.broadcasted_iota(i32, (128, cap), 0) + start
        for r in range(2):
            sel[pl.ds(start, 128), r * cap : (r + 1) * cap] = jnp.where(
                rows == lists[r : r + 1], 1.0, 0.0
            ).astype(bf16)
        return carry

    lax.fori_loop(0, N // 128, sel_body, 0)
    pl.semaphore_wait(barrier, (D - 1) + (B - 1 if gram else 0))

    mm_copies = []
    for o in range(1, D):
        copy = remote(
            mm.at[0], mm.at[o], mm_ss.at[o - 1], mm_rs.at[o - 1], {"domain": lax.rem(d + o, D)}
        )
        copy.start()
        mm_copies.append(copy)

    up = lax.rem(d + 1, D)
    down = lax.rem(d + D - 1, D)

    def halo_copies(step):
        return (
            remote(sent.at[step, 0], halo.at[step, 0], h_ss.at[step, 0], h_rs.at[step, 0], {"domain": up}),
            remote(sent.at[step, 1], halo.at[step, 1], h_ss.at[step, 1], h_rs.at[step, 1], {"domain": down}),
        )

    def send_halo(step, stacked):
        both = jnp.dot(stacked, sel[...], preferred_element_type=f32)
        rows = both[:R] + both[R:]
        sent[step, 0] = rows[:, :cap]
        sent[step, 1] = rows[:, cap:]
        upward, downward = halo_copies(step)
        pl.when(d < D - 1)(upward.start)
        pl.when(d > 0)(downward.start)

    def recv_halo(step):
        upward, downward = halo_copies(step)
        pl.when(d > 0)(upward.wait_recv)
        pl.when(d < D - 1)(downward.wait_recv)
        return jnp.concatenate([halo[step, 0], halo[step, 1]], axis=1)

    def done_halo(step):
        upward, downward = halo_copies(step)
        pl.when(d < D - 1)(upward.wait_send)
        pl.when(d > 0)(downward.wait_send)

    first = jnp.concatenate(split(orb_ref[...]), axis=0)
    send_halo(0, first)

    key = sten_ref[...]
    digit = (key * ((1 << 22) // groups + 1)) >> 22
    slot[...] = key - digit * groups
    unit[...] = jnp.where(digit < DIGITS, jnp.left_shift(1, 4 * jnp.minimum(digit, DIGITS - 1)), 0)

    chunk = 32

    def build(index, carry):
        lane = pl.multiple_of((index % (N // 128)) * 128, 128)
        row = pl.multiple_of((index // (N // 128)) * chunk, chunk)
        rows = lax.broadcasted_iota(i32, (chunk, 128), 0) + row
        acc = [jnp.zeros((chunk, 128), f32) for _ in range(DIGITS)]
        for j in range(6):
            word = jnp.zeros((chunk, 128), i32)
            for i in range(6 * j, 6 * j + 6):
                s = slot[i : i + 1, pl.ds(lane, 128)]
                u = unit[i : i + 1, pl.ds(lane, 128)]
                word = word + jnp.where(rows == s, u, 0)
            for r in range(DIGITS):
                count = (word & (7 << (4 * r))).astype(f32)
                acc[r] = acc[r] + count * (WEIGHTS[j + 1] / WEIGHTS[1] * 2.0 ** (-4 * r))
        for r in range(DIGITS):
            hi, lo = split(acc[r])
            ah[pl.ds(r * groups + row, chunk), pl.ds(lane, 128)] = hi
            al[pl.ds(r * groups + row, chunk), pl.ds(lane, 128)] = lo
        return carry

    lax.fori_loop(0, (N // 128) * (groups // chunk), build, 0)

    for copy in mm_copies:
        copy.wait()
    lowest = mm[0, 0:1, 0:1]
    highest = mm[0, 1:2, 0:1]
    for o in range(1, D):
        lowest = jnp.minimum(lowest, mm[o, 0:1, 0:1])
        highest = jnp.maximum(highest, mm[o, 1:2, 0:1])
    top = highest + SPECTRAL_REACH
    cut = lowest + CUT_SHARE * (top - lowest)
    half_width = (top - cut) / 2.0
    centre = (top + cut) / 2.0
    diagonal = pot - KINETIC * 3.0 * WEIGHTS[0]

    def near(step, stacked):
        total = dot3(stacked, R, ah[:N], al[:N])
        outer = jnp.concatenate(split(recv_halo(step)), axis=0)
        return WEIGHTS[1] * (total + dot3(outer, R, ah[N:], al[N:]))

    sigma = half_width / (lowest - centre)
    scale = 2.0 / sigma
    previous = orb_ref[...]
    factor = sigma / half_width
    current = factor * ((diagonal - centre) * previous - KINETIC * near(0, first))
    for j in range(2, DEGREE + 1):
        stacked = jnp.concatenate(split(current), axis=0)
        send_halo(j - 1, stacked)
        sigma_next = 1.0 / (scale - sigma)
        factor = 2.0 * sigma_next / half_width
        part_two = factor * (diagonal - centre) * current - (sigma * sigma_next) * previous
        following = part_two - (factor * KINETIC) * near(j - 1, stacked)
        previous, current, sigma = current, following, sigma_next
    filt_ref[...] = current
    stacked = jnp.concatenate(split(current), axis=0)
    send_halo(DEGREE, stacked)

    if not gram:
        out_ref[...] = diagonal * current - KINETIC * near(DEGREE, stacked)
        for step in range(DEGREE + 1):
            done_halo(step)
        return

    app, fall, aall, give, core_in, y_in, band_out, band_in = scratch[12:20]
    f_ss, f_rs, a_ss, a_rs, c_ss, c_rs, y_ss, y_rs, b_ss, b_rs = scratch[20:]
    wide = N // B

    def spread(src, dst, ss, rs):
        copies = []
        for o in range(1, B):
            to = lax.rem(b + o, B)
            copy = remote(
                src.at[:, pl.ds(pl.multiple_of(to * wide, wide), wide)],
                dst.at[b],
                ss.at[o - 1],
                rs.at[o - 1],
                {"band": to},
            )
            copy.start()
            copies.append(copy)
        dst[b] = src[:, pl.ds(pl.multiple_of(b * wide, wide), wide)]
        return copies

    f_copies = spread(filt_ref, fall, f_ss, f_rs)
    app[...] = diagonal * current - KINETIC * near(DEGREE, stacked)
    a_copies = spread(app, aall, a_ss, a_rs)
    for copy in f_copies:
        copy.wait_recv()
    orbs = B * R
    left = fall[...].reshape(orbs, wide)
    left_hi, left_lo = split(left)
    left_both = jnp.concatenate([left_hi, left_lo], axis=0)
    for copy in a_copies:
        copy.wait_recv()

    blocks = B // D
    core = lax.rem(d, 2)
    pair = d // 2
    rights = (((1,), (1,)), ((), ()))

    def partial(target):
        start = target * blocks
        right = jnp.concatenate(
            [
                fall[pl.ds(start, blocks)].reshape(blocks * R, wide),
                aall[pl.ds(start, blocks)].reshape(blocks * R, wide),
            ],
            axis=0,
        )
        right_hi, right_lo = split(right)
        both = lax.dot_general(left_both, right_hi, rights, preferred_element_type=f32)
        low = lax.dot_general(left_hi, right_lo, rights, preferred_element_type=f32)
        return both[:orbs] + both[orbs:] + low

    pairs = D // 2
    c_copies = []
    for q in range(pairs):
        turn = lax.rem(pair + 1 + q, pairs)
        give[q] = partial(2 * turn + (1 - core))
        copy = remote(
            give.at[q], core_in.at[q], c_ss.at[q], c_rs.at[q], {"domain": 2 * pair + 1 - core}
        )
        copy.start()
        c_copies.append(copy)
    y_copies = []
    for q in range(pairs):
        turn = lax.rem(pair + 1 + q, pairs)
        own = partial(2 * turn + core)
        c_copies[q].wait_recv()
        core_in[q] = core_in[q] + own
        if q < pairs - 1:
            copy = remote(
                core_in.at[q], y_in.at[q], y_ss.at[q], y_rs.at[q], {"domain": 2 * turn + core}
            )
            copy.start()
            y_copies.append(copy)
    total = core_in[pairs - 1]
    for q in range(pairs - 1):
        y_copies[q].wait_recv()
        total = total + y_in[q]
    band_out[...] = (total * (1.0 / (N * D))).reshape(band_out.shape)
    b_copies = []
    for o in range(1, B):
        to = lax.rem(b + o, B)
        copy = remote(band_out.at[to], band_in.at[o - 1], b_ss.at[o - 1], b_rs.at[o - 1], {"band": to})
        copy.start()
        b_copies.append(copy)
    result = band_out[b]
    for o in range(1, B):
        b_copies[o - 1].wait_recv()
        result = result + band_in[o - 1]
    out_ref[...] = result
    for step in range(DEGREE + 1):
        done_halo(step)
    for copy in f_copies + a_copies + c_copies + y_copies + b_copies:
        copy.wait_send()


def inner_products(left_block, right_block):
    return lax.dot_general(
        left_block,
        right_block,
        (((1,), (1,)), ((), ())),
        precision=lax.Precision.HIGHEST,
        preferred_element_type=f32,
    )


def shards(orbitals, potential, stencil, send_list, send_count):
    D, B = lax.axis_size("domain"), lax.axis_size("band")
    R, N = orbitals.shape
    cap = send_list.shape[1]
    orbs = R * B
    keys = N + 2 * cap
    gram = D == 4 and N % (128 * B) == 0 and B % D == 0 and 2 * orbs // D == 128
    steps = DEGREE + 1
    dma = pltpu.SemaphoreType.DMA
    scratch = [
        pltpu.VMEM((keys, N), bf16),
        pltpu.VMEM((keys, N), bf16),
        pltpu.VMEM((N, 2 * cap), bf16),
        pltpu.VMEM(stencil.shape, i32),
        pltpu.VMEM(stencil.shape, i32),
        pltpu.VMEM((D, 8, 128), f32),
        pltpu.VMEM((steps, 2, R, cap), f32),
        pltpu.VMEM((steps, 2, R, cap), f32),
        dma((D - 1,)),
        dma((D - 1,)),
        dma((steps, 2)),
        dma((steps, 2)),
    ]
    if gram:
        wide = N // B
        width = 2 * orbs // D
        pairs = D // 2
        scratch += [
            pltpu.VMEM((R, N), f32),
            pltpu.VMEM((B, R, wide), f32),
            pltpu.VMEM((B, R, wide), f32),
            pltpu.VMEM((pairs, orbs, width), f32),
            pltpu.VMEM((pairs, orbs, width), f32),
            pltpu.VMEM((pairs - 1, orbs, width), f32),
            pltpu.VMEM((B, R, width), f32),
            pltpu.VMEM((B - 1, R, width), f32),
        ]
        for count in (B - 1, B - 1, pairs, pairs - 1, B - 1):
            scratch += [dma((count,)), dma((count,))]
    second = (R, 2 * orbs // D) if gram else (R, N)
    filtered, other = pl.pallas_call(
        functools.partial(kernel, D, B, gram),
        out_shape=(
            jax.ShapeDtypeStruct((R, N), f32),
            jax.ShapeDtypeStruct(second, f32),
        ),
        in_specs=[pl.BlockSpec(memory_space=pltpu.VMEM)] * 5,
        out_specs=[pl.BlockSpec(memory_space=pltpu.VMEM)] * 2,
        scratch_shapes=scratch,
        compiler_params=pltpu.CompilerParams(
            collective_id=0, has_side_effects=True, vmem_limit_bytes=48 * 1024 * 1024
        ),
    )(orbitals, potential.reshape(1, N), stencil, send_list, send_count)
    if gram:
        half = orbs // D
        return filtered, other[:, :half], other[:, half:]
    results = []
    for block in (filtered, other):
        whole = lax.all_gather(block, "band", axis=0, tiled=True)
        share = inner_products(filtered, whole)
        total = lax.psum_scatter(share, "domain", scatter_dimension=1, tiled=True)
        results.append(total / (N * D))
    return filtered, results[0], results[1]


def solution(mesh):
    placed = (
        P("band", "domain"),
        P("domain"),
        P(None, "domain"),
        P(None, "domain"),
        P(None, "domain"),
    )
    return jax.shard_map(
        shards,
        mesh=mesh,
        in_specs=placed,
        out_specs=(P("band", "domain"), P("band", "domain"), P("band", "domain")),
        check_vma=False,
    )
```

```python
import functools

import jax
import jax.numpy as jnp
from jax import lax
from jax.experimental import pallas as pl
from jax.experimental.pallas import tpu as pltpu
from jax.sharding import PartitionSpec as P

DEGREE = 4
WEIGHTS = (
    -5369.0 / 1800.0,
    12.0 / 7.0,
    -15.0 / 56.0,
    10.0 / 189.0,
    -1.0 / 112.0,
    2.0 / 1925.0,
    -1.0 / 16632.0,
)
KINETIC = 50.0 / 9.0
CUT_SHARE = 0.1
SPECTRAL_REACH = KINETIC * 3.0 * (abs(WEIGHTS[0]) + 2.0 * sum(abs(w) for w in WEIGHTS[1:]))
MESH = pl.DeviceIdType.MESH
DIGITS = 8
f32, bf16, i32 = jnp.float32, jnp.bfloat16, jnp.int32


def remote(src, dst, send_sem, recv_sem, device_id):
    return pltpu.make_async_remote_copy(
        src_ref=src,
        dst_ref=dst,
        send_sem=send_sem,
        recv_sem=recv_sem,
        device_id=device_id,
        device_id_type=MESH,
    )


def split(x):
    hi = x.astype(bf16)
    lo = (x - hi.astype(f32)).astype(bf16)
    return hi, lo


def dot3(stacked, hi_rows, right_hi, right_lo):
    both = jnp.dot(stacked, right_hi, preferred_element_type=f32)
    low = jnp.dot(stacked[:hi_rows], right_lo, preferred_element_type=f32)
    return both[:hi_rows] + both[hi_rows:] + low


def kernel(D, B, gram, orb_in, pot_in, sten_in, list_in, count_ref, filt_ref, out_ref, *scratch):
    orb_ref, pot_ref, sten_ref, list_ref, in_sem = scratch[:5]
    scratch = scratch[5:]
    ah, al, sel, slot, unit, mm, sent, halo, mm_ss, mm_rs, h_ss, h_rs = scratch[:12]
    fetches = [
        pltpu.make_async_copy(source, target, in_sem.at[n])
        for n, (source, target) in enumerate(
            ((list_in, list_ref), (pot_in, pot_ref), (orb_in, orb_ref), (sten_in, sten_ref))
        )
    ]
    for fetch in fetches:
        fetch.start()
    d = lax.axis_index("domain")
    b = lax.axis_index("band")
    R, N = orb_ref.shape
    cap = list_ref.shape[1]
    groups = (N + 2 * cap) // DIGITS

    halo[...] = jnp.zeros_like(halo)
    barrier = pltpu.get_barrier_semaphore()
    for o in range(1, D):
        pl.semaphore_signal(
            barrier, inc=1, device_id={"domain": lax.rem(d + o, D)}, device_id_type=MESH
        )
    if gram:
        for o in range(1, B):
            pl.semaphore_signal(
                barrier, inc=1, device_id={"band": lax.rem(b + o, B)}, device_id_type=MESH
            )

    for fetch in fetches[:2]:
        fetch.wait()
    pot = pot_ref[...]
    mm[0, 0:1] = jnp.broadcast_to(jnp.min(pot, axis=1, keepdims=True), (1, 128))
    mm[0, 1:2] = jnp.broadcast_to(jnp.max(pot, axis=1, keepdims=True), (1, 128))
    live = lax.broadcasted_iota(i32, (2, cap), 1) < count_ref[...]
    lists = jnp.where(live, list_ref[...], -1)

    def sel_body(step, carry):
        start = pl.multiple_of(step * 128, 128)
        rows = lax.broadcasted_iota(i32, (128, cap), 0) + start
        for r in range(2):
            sel[pl.ds(start, 128), r * cap : (r + 1) * cap] = jnp.where(
                rows == lists[r : r + 1], 1.0, 0.0
            ).astype(bf16)
        return carry

    lax.fori_loop(0, N // 128, sel_body, 0)
    pl.semaphore_wait(barrier, (D - 1) + (B - 1 if gram else 0))

    mm_copies = []
    for o in range(1, D):
        copy = remote(
            mm.at[0], mm.at[o], mm_ss.at[o - 1], mm_rs.at[o - 1], {"domain": lax.rem(d + o, D)}
        )
        copy.start()
        mm_copies.append(copy)

    up = lax.rem(d + 1, D)
    down = lax.rem(d + D - 1, D)

    def halo_copies(step):
        return (
            remote(sent.at[step, 0], halo.at[step, 0], h_ss.at[step, 0], h_rs.at[step, 0], {"domain": up}),
            remote(sent.at[step, 1], halo.at[step, 1], h_ss.at[step, 1], h_rs.at[step, 1], {"domain": down}),
        )

    def send_halo(step, stacked):
        both = jnp.dot(stacked, sel[...], preferred_element_type=f32)
        rows = both[:R] + both[R:]
        sent[step, 0] = rows[:, :cap]
        sent[step, 1] = rows[:, cap:]
        upward, downward = halo_copies(step)
        pl.when(d < D - 1)(upward.start)
        pl.when(d > 0)(downward.start)

    def recv_halo(step):
        upward, downward = halo_copies(step)
        pl.when(d > 0)(upward.wait_recv)
        pl.when(d < D - 1)(downward.wait_recv)
        return jnp.concatenate([halo[step, 0], halo[step, 1]], axis=1)

    def done_halo(step):
        upward, downward = halo_copies(step)
        pl.when(d < D - 1)(upward.wait_send)
        pl.when(d > 0)(downward.wait_send)

    fetches[2].wait()
    first = jnp.concatenate(split(orb_ref[...]), axis=0)
    send_halo(0, first)

    fetches[3].wait()
    key = sten_ref[...]
    digit = (key * ((1 << 22) // groups + 1)) >> 22
    slot[...] = key - digit * groups
    unit[...] = jnp.where(digit < DIGITS, jnp.left_shift(1, 4 * jnp.minimum(digit, DIGITS - 1)), 0)

    chunk = 32

    def build(index, carry):
        lane = pl.multiple_of((index % (N // 128)) * 128, 128)
        row = pl.multiple_of((index // (N // 128)) * chunk, chunk)
        rows = lax.broadcasted_iota(i32, (chunk, 128), 0) + row
        acc = [jnp.zeros((chunk, 128), f32) for _ in range(DIGITS)]
        for j in range(6):
            word = jnp.zeros((chunk, 128), i32)
            for i in range(6 * j, 6 * j + 6):
                s = slot[i : i + 1, pl.ds(lane, 128)]
                u = unit[i : i + 1, pl.ds(lane, 128)]
                word = word + jnp.where(rows == s, u, 0)
            for r in range(DIGITS):
                count = (word & (7 << (4 * r))).astype(f32)
                acc[r] = acc[r] + count * (WEIGHTS[j + 1] / WEIGHTS[1] * 2.0 ** (-4 * r))
        for r in range(DIGITS):
            hi, lo = split(acc[r])
            ah[pl.ds(r * groups + row, chunk), pl.ds(lane, 128)] = hi
            al[pl.ds(r * groups + row, chunk), pl.ds(lane, 128)] = lo
        return carry

    lax.fori_loop(0, (N // 128) * (groups // chunk), build, 0)

    for copy in mm_copies:
        copy.wait()
    lowest = mm[0, 0:1, 0:1]
    highest = mm[0, 1:2, 0:1]
    for o in range(1, D):
        lowest = jnp.minimum(lowest, mm[o, 0:1, 0:1])
        highest = jnp.maximum(highest, mm[o, 1:2, 0:1])
    top = highest + SPECTRAL_REACH
    cut = lowest + CUT_SHARE * (top - lowest)
    half_width = (top - cut) / 2.0
    centre = (top + cut) / 2.0
    diagonal = pot - KINETIC * 3.0 * WEIGHTS[0]

    def near(step, stacked):
        total = dot3(stacked, R, ah[:N], al[:N])
        outer = jnp.concatenate(split(recv_halo(step)), axis=0)
        return WEIGHTS[1] * (total + dot3(outer, R, ah[N:], al[N:]))

    sigma = half_width / (lowest - centre)
    scale = 2.0 / sigma
    previous = orb_ref[...]
    factor = sigma / half_width
    current = factor * ((diagonal - centre) * previous - KINETIC * near(0, first))
    for j in range(2, DEGREE + 1):
        stacked = jnp.concatenate(split(current), axis=0)
        send_halo(j - 1, stacked)
        sigma_next = 1.0 / (scale - sigma)
        factor = 2.0 * sigma_next / half_width
        part_two = factor * (diagonal - centre) * current - (sigma * sigma_next) * previous
        following = part_two - (factor * KINETIC) * near(j - 1, stacked)
        previous, current, sigma = current, following, sigma_next
    filt_ref[...] = current
    stacked = jnp.concatenate(split(current), axis=0)
    send_halo(DEGREE, stacked)

    if not gram:
        out_ref[...] = diagonal * current - KINETIC * near(DEGREE, stacked)
        for step in range(DEGREE + 1):
            done_halo(step)
        return

    app, fall, aall, give, keep, core_in, y_in, band_out, band_in = scratch[12:21]
    f_ss, f_rs, a_ss, a_rs, c_ss, c_rs, y_ss, y_rs, b_ss, b_rs = scratch[21:]
    wide = N // B

    def spread(src, dst, ss, rs):
        copies = []
        for o in range(1, B):
            to = lax.rem(b + o, B)
            copy = remote(
                src.at[:, pl.ds(pl.multiple_of(to * wide, wide), wide)],
                dst.at[b],
                ss.at[o - 1],
                rs.at[o - 1],
                {"band": to},
            )
            copy.start()
            copies.append(copy)
        dst[b] = src[:, pl.ds(pl.multiple_of(b * wide, wide), wide)]
        return copies

    f_copies = spread(filt_ref, fall, f_ss, f_rs)
    app[...] = diagonal * current - KINETIC * near(DEGREE, stacked)
    a_copies = spread(app, aall, a_ss, a_rs)
    for copy in f_copies:
        copy.wait_recv()
    orbs = B * R
    left = fall[...].reshape(orbs, wide)
    left_hi, left_lo = split(left)
    left_both = jnp.concatenate([left_hi, left_lo], axis=0)
    for copy in a_copies:
        copy.wait_recv()

    blocks = B // D
    core = lax.rem(d, 2)
    pair = d // 2
    rights = (((1,), (1,)), ((), ()))

    def partial(target):
        start = target * blocks
        right = jnp.concatenate(
            [
                fall[pl.ds(start, blocks)].reshape(blocks * R, wide),
                aall[pl.ds(start, blocks)].reshape(blocks * R, wide),
            ],
            axis=0,
        )
        right_hi, right_lo = split(right)
        both = lax.dot_general(left_both, right_hi, rights, preferred_element_type=f32)
        low = lax.dot_general(left_hi, right_lo, rights, preferred_element_type=f32)
        return both[:orbs] + both[orbs:] + low

    pairs = D // 2
    chunks = D
    per = B // chunks
    height = per * R
    order = [lax.rem(b // per + 1 + i, chunks) for i in range(chunks)]
    spans = [pl.ds(pl.multiple_of(h * height, height), height) for h in order]
    c_copies = []
    for q in range(pairs):
        turn = lax.rem(pair + 1 + q, pairs)
        give[q] = partial(2 * turn + (1 - core))
        row = []
        for i in range(chunks):
            copy = remote(
                give.at[q, spans[i]],
                core_in.at[q, spans[i]],
                c_ss.at[q, i],
                c_rs.at[q, i],
                {"domain": 2 * pair + 1 - core},
            )
            copy.start()
            row.append(copy)
        c_copies.append(row)
    for q in range(pairs):
        keep[q] = partial(2 * lax.rem(pair + 1 + q, pairs) + core)
    y_copies = []
    for q in range(pairs - 1):
        turn = lax.rem(pair + 1 + q, pairs)
        row = []
        for i in range(chunks):
            c_copies[q][i].wait_recv()
            keep[q, spans[i]] = keep[q, spans[i]] + core_in[q, spans[i]]
            copy = remote(
                keep.at[q, spans[i]],
                y_in.at[q, spans[i]],
                y_ss.at[q, i],
                y_rs.at[q, i],
                {"domain": 2 * turn + core},
            )
            copy.start()
            row.append(copy)
        y_copies.append(row)

    def band_copy(to):
        return remote(band_out.at[to], band_in.at[b], b_ss.at[to], b_rs.at[b], {"band": to})

    for i in range(chunks):
        c_copies[pairs - 1][i].wait_recv()
        total = keep[pairs - 1, spans[i]] + core_in[pairs - 1, spans[i]]
        for q in range(pairs - 1):
            y_copies[q][i].wait_recv()
            total = total + y_in[q, spans[i]]
        total = total * (1.0 / (N * D))
        for t in range(per):
            to = order[i] * per + t
            band_out[to] = total[t * R : (t + 1) * R]
            pl.when(to != b)(band_copy(to).start)
    result = band_out[b]
    for o in range(1, B):
        other = lax.rem(b + o, B)
        remote(
            band_out.at[other], band_in.at[other], b_ss.at[other], b_rs.at[other], {"band": other}
        ).wait_recv()
        result = result + band_in[other]
    out_ref[...] = result
    for o in range(1, B):
        band_copy(lax.rem(b + o, B)).wait_send()
    for step in range(DEGREE + 1):
        done_halo(step)
    for copy in f_copies + a_copies + sum(c_copies + y_copies, []):
        copy.wait_send()


def inner_products(left_block, right_block):
    return lax.dot_general(
        left_block,
        right_block,
        (((1,), (1,)), ((), ())),
        precision=lax.Precision.HIGHEST,
        preferred_element_type=f32,
    )


def shards(orbitals, potential, stencil, send_list, send_count):
    D, B = lax.axis_size("domain"), lax.axis_size("band")
    R, N = orbitals.shape
    cap = send_list.shape[1]
    orbs = R * B
    keys = N + 2 * cap
    gram = D == 4 and N % (128 * B) == 0 and B % D == 0 and 2 * orbs // D == 128
    steps = DEGREE + 1
    dma = pltpu.SemaphoreType.DMA
    scratch = [
        pltpu.VMEM((R, N), f32),
        pltpu.VMEM((1, N), f32),
        pltpu.VMEM(stencil.shape, i32),
        pltpu.VMEM(send_list.shape, i32),
        dma((4,)),
        pltpu.VMEM((keys, N), bf16),
        pltpu.VMEM((keys, N), bf16),
        pltpu.VMEM((N, 2 * cap), bf16),
        pltpu.VMEM(stencil.shape, i32),
        pltpu.VMEM(stencil.shape, i32),
        pltpu.VMEM((D, 8, 128), f32),
        pltpu.VMEM((steps, 2, R, cap), f32),
        pltpu.VMEM((steps, 2, R, cap), f32),
        dma((D - 1,)),
        dma((D - 1,)),
        dma((steps, 2)),
        dma((steps, 2)),
    ]
    if gram:
        wide = N // B
        width = 2 * orbs // D
        pairs = D // 2
        scratch += [
            pltpu.VMEM((R, N), f32),
            pltpu.VMEM((B, R, wide), f32),
            pltpu.VMEM((B, R, wide), f32),
            pltpu.VMEM((pairs, orbs, width), f32),
            pltpu.VMEM((pairs, orbs, width), f32),
            pltpu.VMEM((pairs, orbs, width), f32),
            pltpu.VMEM((pairs - 1, orbs, width), f32),
            pltpu.VMEM((B, R, width), f32),
            pltpu.VMEM((B, R, width), f32),
        ]
        for counts in ((B - 1,), (B - 1,), (pairs, D), (pairs - 1, D), (B,)):
            scratch += [dma(counts), dma(counts)]
    second = (R, 2 * orbs // D) if gram else (R, N)
    filtered, other = pl.pallas_call(
        functools.partial(kernel, D, B, gram),
        out_shape=(
            jax.ShapeDtypeStruct((R, N), f32),
            jax.ShapeDtypeStruct(second, f32),
        ),
        in_specs=[pl.BlockSpec(memory_space=pl.ANY)] * 4
        + [pl.BlockSpec(memory_space=pltpu.VMEM)],
        out_specs=[pl.BlockSpec(memory_space=pltpu.VMEM)] * 2,
        scratch_shapes=scratch,
        compiler_params=pltpu.CompilerParams(
            collective_id=0, has_side_effects=True, vmem_limit_bytes=48 * 1024 * 1024
        ),
    )(orbitals, potential.reshape(1, N), stencil, send_list, send_count)
    if gram:
        half = orbs // D
        return filtered, other[:, :half], other[:, half:]
    results = []
    for block in (filtered, other):
        whole = lax.all_gather(block, "band", axis=0, tiled=True)
        share = inner_products(filtered, whole)
        total = lax.psum_scatter(share, "domain", scatter_dimension=1, tiled=True)
        results.append(total / (N * D))
    return filtered, results[0], results[1]


def solution(mesh):
    placed = (
        P("band", "domain"),
        P("domain"),
        P(None, "domain"),
        P(None, "domain"),
        P(None, "domain"),
    )
    return jax.shard_map(
        shards,
        mesh=mesh,
        in_specs=placed,
        out_specs=(P("band", "domain"), P("band", "domain"), P("band", "domain")),
        check_vma=False,
    )
```

```python
import functools

import jax
import jax.numpy as jnp
from jax import lax
from jax.experimental import pallas as pl
from jax.experimental.pallas import tpu as pltpu
from jax.sharding import PartitionSpec as P

DEGREE = 4
WEIGHTS = (
    -5369.0 / 1800.0,
    12.0 / 7.0,
    -15.0 / 56.0,
    10.0 / 189.0,
    -1.0 / 112.0,
    2.0 / 1925.0,
    -1.0 / 16632.0,
)
KINETIC = 50.0 / 9.0
CUT_SHARE = 0.1
SPECTRAL_REACH = KINETIC * 3.0 * (abs(WEIGHTS[0]) + 2.0 * sum(abs(w) for w in WEIGHTS[1:]))
MESH = pl.DeviceIdType.MESH
DIGITS = 8
f32, bf16, i32 = jnp.float32, jnp.bfloat16, jnp.int32


def remote(src, dst, send_sem, recv_sem, device_id):
    return pltpu.make_async_remote_copy(
        src_ref=src,
        dst_ref=dst,
        send_sem=send_sem,
        recv_sem=recv_sem,
        device_id=device_id,
        device_id_type=MESH,
    )


def split(x):
    hi = x.astype(bf16)
    lo = (x - hi.astype(f32)).astype(bf16)
    return hi, lo


def dot3(stacked, hi_rows, right_hi, right_lo):
    both = jnp.dot(stacked, right_hi, preferred_element_type=f32)
    low = jnp.dot(stacked[:hi_rows], right_lo, preferred_element_type=f32)
    return both[:hi_rows] + both[hi_rows:] + low


def kernel(D, B, gram, orb_in, pot_in, sten_in, list_in, count_ref, filt_ref, out_ref, *scratch):
    orb_ref, pot_ref, sten_ref, list_ref, in_sem = scratch[:5]
    scratch = scratch[5:]
    ah, al, sel, slot, unit, mm, sent, halo, mm_ss, mm_rs, h_ss, h_rs = scratch[:12]
    fetches = [
        pltpu.make_async_copy(source, target, in_sem.at[n])
        for n, (source, target) in enumerate(
            ((list_in, list_ref), (pot_in, pot_ref), (orb_in, orb_ref), (sten_in, sten_ref))
        )
    ]
    for fetch in fetches:
        fetch.start()
    d = lax.axis_index("domain")
    b = lax.axis_index("band")
    R, N = orb_ref.shape
    cap = list_ref.shape[1]
    groups = (N + 2 * cap) // DIGITS

    halo[...] = jnp.zeros_like(halo)
    barrier = pltpu.get_barrier_semaphore()
    for o in range(1, D):
        pl.semaphore_signal(
            barrier, inc=1, device_id={"domain": lax.rem(d + o, D)}, device_id_type=MESH
        )
    if gram:
        for o in range(1, B):
            pl.semaphore_signal(
                barrier, inc=1, device_id={"band": lax.rem(b + o, B)}, device_id_type=MESH
            )

    for fetch in fetches[:2]:
        fetch.wait()
    pot = pot_ref[...]
    mm[0, 0:1] = jnp.broadcast_to(jnp.min(pot, axis=1, keepdims=True), (1, 128))
    mm[0, 1:2] = jnp.broadcast_to(jnp.max(pot, axis=1, keepdims=True), (1, 128))
    live = lax.broadcasted_iota(i32, (2, cap), 1) < count_ref[...]
    lists = jnp.where(live, list_ref[...], -1)

    def sel_body(step, carry):
        start = pl.multiple_of(step * 128, 128)
        rows = lax.broadcasted_iota(i32, (128, cap), 0) + start
        for r in range(2):
            sel[pl.ds(start, 128), r * cap : (r + 1) * cap] = jnp.where(
                rows == lists[r : r + 1], 1.0, 0.0
            ).astype(bf16)
        return carry

    lax.fori_loop(0, N // 128, sel_body, 0)
    pl.semaphore_wait(barrier, (D - 1) + (B - 1 if gram else 0))

    mm_copies = []
    for o in range(1, D):
        copy = remote(
            mm.at[0], mm.at[o], mm_ss.at[o - 1], mm_rs.at[o - 1], {"domain": lax.rem(d + o, D)}
        )
        copy.start()
        mm_copies.append(copy)

    up = lax.rem(d + 1, D)
    down = lax.rem(d + D - 1, D)

    def halo_copies(step):
        return (
            remote(sent.at[step, 0], halo.at[step, 0], h_ss.at[step, 0], h_rs.at[step, 0], {"domain": up}),
            remote(sent.at[step, 1], halo.at[step, 1], h_ss.at[step, 1], h_rs.at[step, 1], {"domain": down}),
        )

    def send_halo(step, stacked):
        both = jnp.dot(stacked, sel[...], preferred_element_type=f32)
        rows = both[:R] + both[R:]
        sent[step, 0] = rows[:, :cap]
        sent[step, 1] = rows[:, cap:]
        upward, downward = halo_copies(step)
        pl.when(d < D - 1)(upward.start)
        pl.when(d > 0)(downward.start)

    def recv_halo(step):
        upward, downward = halo_copies(step)
        pl.when(d > 0)(upward.wait_recv)
        pl.when(d < D - 1)(downward.wait_recv)
        return jnp.concatenate([halo[step, 0], halo[step, 1]], axis=1)

    def done_halo(step):
        upward, downward = halo_copies(step)
        pl.when(d < D - 1)(upward.wait_send)
        pl.when(d > 0)(downward.wait_send)

    fetches[2].wait()
    first = jnp.concatenate(split(orb_ref[...]), axis=0)
    send_halo(0, first)

    fetches[3].wait()
    key = sten_ref[...]
    digit = (key * ((1 << 22) // groups + 1)) >> 22
    slot[...] = key - digit * groups
    unit[...] = jnp.where(digit < DIGITS, jnp.left_shift(1, 4 * jnp.minimum(digit, DIGITS - 1)), 0)

    chunk = 32

    def build(index, carry):
        lane = pl.multiple_of((index % (N // 128)) * 128, 128)
        row = pl.multiple_of((index // (N // 128)) * chunk, chunk)
        rows = lax.broadcasted_iota(i32, (chunk, 128), 0) + row
        acc = [jnp.zeros((chunk, 128), f32) for _ in range(DIGITS)]
        for j in range(6):
            word = jnp.zeros((chunk, 128), i32)
            for i in range(6 * j, 6 * j + 6):
                s = slot[i : i + 1, pl.ds(lane, 128)]
                u = unit[i : i + 1, pl.ds(lane, 128)]
                word = word + jnp.where(rows == s, u, 0)
            for r in range(DIGITS):
                count = (word & (7 << (4 * r))).astype(f32)
                acc[r] = acc[r] + count * (WEIGHTS[j + 1] / WEIGHTS[1] * 2.0 ** (-4 * r))
        for r in range(DIGITS):
            hi, lo = split(acc[r])
            ah[pl.ds(r * groups + row, chunk), pl.ds(lane, 128)] = hi
            al[pl.ds(r * groups + row, chunk), pl.ds(lane, 128)] = lo
        return carry

    lax.fori_loop(0, (N // 128) * (groups // chunk), build, 0)

    for copy in mm_copies:
        copy.wait()
    lowest = mm[0, 0:1, 0:1]
    highest = mm[0, 1:2, 0:1]
    for o in range(1, D):
        lowest = jnp.minimum(lowest, mm[o, 0:1, 0:1])
        highest = jnp.maximum(highest, mm[o, 1:2, 0:1])
    top = highest + SPECTRAL_REACH
    cut = lowest + CUT_SHARE * (top - lowest)
    half_width = (top - cut) / 2.0
    centre = (top + cut) / 2.0
    diagonal = pot - KINETIC * 3.0 * WEIGHTS[0]

    def near(step, stacked):
        total = dot3(stacked, R, ah[:N], al[:N])
        outer = jnp.concatenate(split(recv_halo(step)), axis=0)
        return WEIGHTS[1] * (total + dot3(outer, R, ah[N:], al[N:]))

    sigma = half_width / (lowest - centre)
    scale = 2.0 / sigma
    previous = orb_ref[...]
    factor = sigma / half_width
    current = factor * ((diagonal - centre) * previous - KINETIC * near(0, first))
    for j in range(2, DEGREE + 1):
        stacked = jnp.concatenate(split(current), axis=0)
        send_halo(j - 1, stacked)
        sigma_next = 1.0 / (scale - sigma)
        factor = 2.0 * sigma_next / half_width
        part_two = factor * (diagonal - centre) * current - (sigma * sigma_next) * previous
        following = part_two - (factor * KINETIC) * near(j - 1, stacked)
        previous, current, sigma = current, following, sigma_next
    filt_ref[...] = current
    stacked = jnp.concatenate(split(current), axis=0)
    send_halo(DEGREE, stacked)

    if not gram:
        out_ref[...] = diagonal * current - KINETIC * near(DEGREE, stacked)
        for step in range(DEGREE + 1):
            done_halo(step)
        return

    app, fall, aall, give, keep, core_in, y_in, band_out, band_in = scratch[12:21]
    f_ss, f_rs, a_ss, a_rs, c_ss, c_rs, y_ss, y_rs, b_ss, b_rs = scratch[21:]
    wide = N // B

    def spread(src, dst, ss, rs):
        copies = []
        for o in range(1, B):
            to = lax.rem(b + o, B)
            copy = remote(
                src.at[:, pl.ds(pl.multiple_of(to * wide, wide), wide)],
                dst.at[b],
                ss.at[o - 1],
                rs.at[o - 1],
                {"band": to},
            )
            copy.start()
            copies.append(copy)
        dst[b] = src[:, pl.ds(pl.multiple_of(b * wide, wide), wide)]
        return copies

    f_copies = spread(filt_ref, fall, f_ss, f_rs)
    app[...] = diagonal * current - KINETIC * near(DEGREE, stacked)
    a_copies = spread(app, aall, a_ss, a_rs)
    for copy in f_copies:
        copy.wait_recv()
    orbs = B * R
    left = fall[...].reshape(orbs, wide)
    left_hi, left_lo = split(left)
    left_both = jnp.concatenate([left_hi, left_lo], axis=0)
    for copy in a_copies:
        copy.wait_recv()

    blocks = B // D
    core = lax.rem(d, 2)
    pair = d // 2
    rights = (((1,), (1,)), ((), ()))

    def partial(target):
        start = target * blocks
        right = jnp.concatenate(
            [
                fall[pl.ds(start, blocks)].reshape(blocks * R, wide),
                aall[pl.ds(start, blocks)].reshape(blocks * R, wide),
            ],
            axis=0,
        )
        right_hi, right_lo = split(right)
        both = lax.dot_general(left_both, right_hi, rights, preferred_element_type=f32)
        low = lax.dot_general(left_hi, right_lo, rights, preferred_element_type=f32)
        return both[:orbs] + both[orbs:] + low

    pairs = D // 2
    chunks = D
    per = B // chunks
    height = per * R
    order = [lax.rem(b // per + 1 + i, chunks) for i in range(chunks)]
    spans = [pl.ds(pl.multiple_of(h * height, height), height) for h in order]
    c_copies = []
    for q in range(pairs):
        turn = lax.rem(pair + 1 + q, pairs)
        give[q] = partial(2 * turn + (1 - core))
        row = []
        for i in range(chunks):
            copy = remote(
                give.at[q, spans[i]],
                core_in.at[q, spans[i]],
                c_ss.at[q, i],
                c_rs.at[q, i],
                {"domain": 2 * pair + 1 - core},
            )
            copy.start()
            row.append(copy)
        c_copies.append(row)
    for q in range(pairs):
        keep[q] = partial(2 * lax.rem(pair + 1 + q, pairs) + core)
    y_copies = []
    for q in range(pairs - 1):
        turn = lax.rem(pair + 1 + q, pairs)
        row = []
        for i in range(chunks):
            c_copies[q][i].wait_recv()
            keep[q, spans[i]] = keep[q, spans[i]] + core_in[q, spans[i]]
            copy = remote(
                keep.at[q, spans[i]],
                y_in.at[q, spans[i]],
                y_ss.at[q, i],
                y_rs.at[q, i],
                {"domain": 2 * turn + core},
            )
            copy.start()
            row.append(copy)
        y_copies.append(row)

    def band_copy(to):
        return remote(band_out.at[to], band_in.at[b], b_ss.at[to], b_rs.at[b], {"band": to})

    for i in range(chunks):
        c_copies[pairs - 1][i].wait_recv()
        total = keep[pairs - 1, spans[i]] + core_in[pairs - 1, spans[i]]
        for q in range(pairs - 1):
            y_copies[q][i].wait_recv()
            total = total + y_in[q, spans[i]]
        total = total * (1.0 / (N * D))
        for t in range(per):
            to = order[i] * per + t
            band_out[to] = total[t * R : (t + 1) * R]
            pl.when(to != b)(band_copy(to).start)
    result = band_out[b]
    for o in range(1, B):
        other = lax.rem(b + o, B)
        remote(
            band_out.at[other], band_in.at[other], b_ss.at[other], b_rs.at[other], {"band": other}
        ).wait_recv()
        result = result + band_in[other]
    out_ref[...] = result
    for o in range(1, B):
        band_copy(lax.rem(b + o, B)).wait_send()
    for step in range(DEGREE + 1):
        done_halo(step)
    for copy in f_copies + a_copies + sum(c_copies + y_copies, []):
        copy.wait_send()


def inner_products(left_block, right_block):
    return lax.dot_general(
        left_block,
        right_block,
        (((1,), (1,)), ((), ())),
        precision=lax.Precision.HIGHEST,
        preferred_element_type=f32,
    )


def shards(orbitals, potential, stencil, send_list, send_count):
    D, B = lax.axis_size("domain"), lax.axis_size("band")
    R, N = orbitals.shape
    cap = send_list.shape[1]
    orbs = R * B
    keys = N + 2 * cap
    gram = D == 4 and N % (128 * B) == 0 and B % D == 0 and 2 * orbs // D == 128
    steps = DEGREE + 1
    dma = pltpu.SemaphoreType.DMA
    scratch = [
        pltpu.VMEM((R, N), f32),
        pltpu.VMEM((1, N), f32),
        pltpu.VMEM(stencil.shape, i32),
        pltpu.VMEM(send_list.shape, i32),
        dma((4,)),
        pltpu.VMEM((keys, N), bf16),
        pltpu.VMEM((keys, N), bf16),
        pltpu.VMEM((N, 2 * cap), bf16),
        pltpu.VMEM(stencil.shape, i32),
        pltpu.VMEM(stencil.shape, i32),
        pltpu.VMEM((D, 8, 128), f32),
        pltpu.VMEM((steps, 2, R, cap), f32),
        pltpu.VMEM((steps, 2, R, cap), f32),
        dma((D - 1,)),
        dma((D - 1,)),
        dma((steps, 2)),
        dma((steps, 2)),
    ]
    if gram:
        wide = N // B
        width = 2 * orbs // D
        pairs = D // 2
        scratch += [
            pltpu.VMEM((R, N), f32),
            pltpu.VMEM((B, R, wide), f32),
            pltpu.VMEM((B, R, wide), f32),
            pltpu.VMEM((pairs, orbs, width), f32),
            pltpu.VMEM((pairs, orbs, width), f32),
            pltpu.VMEM((pairs, orbs, width), f32),
            pltpu.VMEM((pairs - 1, orbs, width), f32),
            pltpu.VMEM((B, R, width), f32),
            pltpu.VMEM((B, R, width), f32),
        ]
        for counts in ((B - 1,), (B - 1,), (pairs, D), (pairs - 1, D), (B,)):
            scratch += [dma(counts), dma(counts)]
    second = (R, 2 * orbs // D) if gram else (R, N)
    filtered, other = pl.pallas_call(
        functools.partial(kernel, D, B, gram),
        out_shape=(
            jax.ShapeDtypeStruct((R, N), f32),
            jax.ShapeDtypeStruct(second, f32),
        ),
        in_specs=[pl.BlockSpec(memory_space=pltpu.HBM)] * 4
        + [pl.BlockSpec(memory_space=pltpu.VMEM)],
        out_specs=[pl.BlockSpec(memory_space=pltpu.VMEM)] * 2,
        scratch_shapes=scratch,
        compiler_params=pltpu.CompilerParams(
            collective_id=0, has_side_effects=True, vmem_limit_bytes=56 * 1024 * 1024
        ),
    )(orbitals, potential.reshape(1, N), stencil, send_list, send_count)
    if gram:
        half = orbs // D
        return filtered, other[:, :half], other[:, half:]
    results = []
    for block in (filtered, other):
        whole = lax.all_gather(block, "band", axis=0, tiled=True)
        share = inner_products(filtered, whole)
        total = lax.psum_scatter(share, "domain", scatter_dimension=1, tiled=True)
        results.append(total / (N * D))
    return filtered, results[0], results[1]


def solution(mesh):
    placed = (
        P("band", "domain"),
        P("domain"),
        P(None, "domain"),
        P(None, "domain"),
        P(None, "domain"),
    )
    return jax.shard_map(
        shards,
        mesh=mesh,
        in_specs=placed,
        out_specs=(P("band", "domain"), P("band", "domain"), P("band", "domain")),
        check_vma=False,
    )
```

```python
import functools

import jax
import jax.numpy as jnp
from jax import lax
from jax.experimental import pallas as pl
from jax.experimental.pallas import tpu as pltpu
from jax.sharding import PartitionSpec as P

DEGREE = 4
WEIGHTS = (
    -5369.0 / 1800.0,
    12.0 / 7.0,
    -15.0 / 56.0,
    10.0 / 189.0,
    -1.0 / 112.0,
    2.0 / 1925.0,
    -1.0 / 16632.0,
)
KINETIC = 50.0 / 9.0
CUT_SHARE = 0.1
SPECTRAL_REACH = KINETIC * 3.0 * (abs(WEIGHTS[0]) + 2.0 * sum(abs(w) for w in WEIGHTS[1:]))
MESH = pl.DeviceIdType.MESH
DIGITS = 8
f32, bf16, i32 = jnp.float32, jnp.bfloat16, jnp.int32


def remote(src, dst, send_sem, recv_sem, device_id):
    return pltpu.make_async_remote_copy(
        src_ref=src,
        dst_ref=dst,
        send_sem=send_sem,
        recv_sem=recv_sem,
        device_id=device_id,
        device_id_type=MESH,
    )


def split(x):
    hi = x.astype(bf16)
    lo = (x - hi.astype(f32)).astype(bf16)
    return hi, lo


def dot3(stacked, hi_rows, right_hi, right_lo):
    both = jnp.dot(stacked, right_hi, preferred_element_type=f32)
    low = jnp.dot(stacked[:hi_rows], right_lo, preferred_element_type=f32)
    return both[:hi_rows] + both[hi_rows:] + low


def kernel(D, B, gram, orb_in, pot_in, sten_in, list_in, count_ref, filt_ref, out_ref, *scratch):
    orb_ref, pot_ref, sten_ref, list_ref, in_sem = scratch[:5]
    scratch = scratch[5:]
    ah, al, sel, slot, unit, mm, sent, halo, mm_ss, mm_rs, h_ss, h_rs = scratch[:12]
    fetches = [
        pltpu.make_async_copy(source, target, in_sem.at[n])
        for n, (source, target) in enumerate(
            ((list_in, list_ref), (pot_in, pot_ref), (orb_in, orb_ref), (sten_in, sten_ref))
        )
    ]
    for fetch in fetches:
        fetch.start()
    d = lax.axis_index("domain")
    b = lax.axis_index("band")
    R, N = orb_ref.shape
    cap = list_ref.shape[1]
    groups = (N + 2 * cap) // DIGITS

    halo[...] = jnp.zeros_like(halo)
    barrier = pltpu.get_barrier_semaphore()
    for o in range(1, D):
        pl.semaphore_signal(
            barrier, inc=1, device_id={"domain": lax.rem(d + o, D)}, device_id_type=MESH
        )
    if gram:
        for o in range(1, B):
            pl.semaphore_signal(
                barrier, inc=1, device_id={"band": lax.rem(b + o, B)}, device_id_type=MESH
            )

    for fetch in fetches[:2]:
        fetch.wait()
    pot = pot_ref[...]
    mm[0, 0:1] = jnp.broadcast_to(jnp.min(pot, axis=1, keepdims=True), (1, 128))
    mm[0, 1:2] = jnp.broadcast_to(jnp.max(pot, axis=1, keepdims=True), (1, 128))
    live = lax.broadcasted_iota(i32, (2, cap), 1) < count_ref[...]
    lists = jnp.where(live, list_ref[...], -1)

    def sel_body(step, carry):
        start = pl.multiple_of(step * 128, 128)
        rows = lax.broadcasted_iota(i32, (128, cap), 0) + start
        for r in range(2):
            sel[pl.ds(start, 128), r * cap : (r + 1) * cap] = jnp.where(
                rows == lists[r : r + 1], 1.0, 0.0
            ).astype(bf16)
        return carry

    lax.fori_loop(0, N // 128, sel_body, 0)
    pl.semaphore_wait(barrier, (D - 1) + (B - 1 if gram else 0))

    mm_copies = []
    for o in range(1, D):
        copy = remote(
            mm.at[0], mm.at[o], mm_ss.at[o - 1], mm_rs.at[o - 1], {"domain": lax.rem(d + o, D)}
        )
        copy.start()
        mm_copies.append(copy)

    up = lax.rem(d + 1, D)
    down = lax.rem(d + D - 1, D)

    def halo_copies(step):
        return (
            remote(sent.at[step, 0], halo.at[step, 0], h_ss.at[step, 0], h_rs.at[step, 0], {"domain": up}),
            remote(sent.at[step, 1], halo.at[step, 1], h_ss.at[step, 1], h_rs.at[step, 1], {"domain": down}),
        )

    def send_halo(step, stacked):
        both = jnp.dot(stacked, sel[...], preferred_element_type=f32)
        rows = both[:R] + both[R:]
        sent[step, 0] = rows[:, :cap]
        sent[step, 1] = rows[:, cap:]
        upward, downward = halo_copies(step)
        pl.when(d < D - 1)(upward.start)
        pl.when(d > 0)(downward.start)

    def recv_halo(step):
        upward, downward = halo_copies(step)
        pl.when(d > 0)(upward.wait_recv)
        pl.when(d < D - 1)(downward.wait_recv)
        return jnp.concatenate([halo[step, 0], halo[step, 1]], axis=1)

    def done_halo(step):
        upward, downward = halo_copies(step)
        pl.when(d < D - 1)(upward.wait_send)
        pl.when(d > 0)(downward.wait_send)

    fetches[2].wait()
    first = jnp.concatenate(split(orb_ref[...]), axis=0)
    send_halo(0, first)

    fetches[3].wait()
    key = sten_ref[...]
    digit = (key * ((1 << 22) // groups + 1)) >> 22
    slot[...] = key - digit * groups
    unit[...] = jnp.where(digit < DIGITS, jnp.left_shift(1, 4 * jnp.minimum(digit, DIGITS - 1)), 0)

    chunk = 32

    def build(index, carry):
        lane = pl.multiple_of((index % (N // 128)) * 128, 128)
        row = pl.multiple_of((index // (N // 128)) * chunk, chunk)
        rows = lax.broadcasted_iota(i32, (chunk, 128), 0) + row
        acc = [jnp.zeros((chunk, 128), f32) for _ in range(DIGITS)]
        for j in range(6):
            word = jnp.zeros((chunk, 128), i32)
            for i in range(6 * j, 6 * j + 6):
                s = slot[i : i + 1, pl.ds(lane, 128)]
                u = unit[i : i + 1, pl.ds(lane, 128)]
                word = word + jnp.where(rows == s, u, 0)
            for r in range(DIGITS):
                count = (word & (7 << (4 * r))).astype(f32)
                acc[r] = acc[r] + count * (WEIGHTS[j + 1] / WEIGHTS[1] * 2.0 ** (-4 * r))
        for r in range(DIGITS):
            hi, lo = split(acc[r])
            ah[pl.ds(r * groups + row, chunk), pl.ds(lane, 128)] = hi
            al[pl.ds(r * groups + row, chunk), pl.ds(lane, 128)] = lo
        return carry

    lax.fori_loop(0, (N // 128) * (groups // chunk), build, 0)

    for copy in mm_copies:
        copy.wait()
    lowest = mm[0, 0:1, 0:1]
    highest = mm[0, 1:2, 0:1]
    for o in range(1, D):
        lowest = jnp.minimum(lowest, mm[o, 0:1, 0:1])
        highest = jnp.maximum(highest, mm[o, 1:2, 0:1])
    top = highest + SPECTRAL_REACH
    cut = lowest + CUT_SHARE * (top - lowest)
    half_width = (top - cut) / 2.0
    centre = (top + cut) / 2.0
    diagonal = pot - KINETIC * 3.0 * WEIGHTS[0]

    def near(step, stacked):
        total = dot3(stacked, R, ah[:N], al[:N])
        outer = jnp.concatenate(split(recv_halo(step)), axis=0)
        return WEIGHTS[1] * (total + dot3(outer, R, ah[N:], al[N:]))

    sigma = half_width / (lowest - centre)
    scale = 2.0 / sigma
    previous = orb_ref[...]
    factor = sigma / half_width
    current = factor * ((diagonal - centre) * previous - KINETIC * near(0, first))
    for j in range(2, DEGREE + 1):
        stacked = jnp.concatenate(split(current), axis=0)
        send_halo(j - 1, stacked)
        sigma_next = 1.0 / (scale - sigma)
        factor = 2.0 * sigma_next / half_width
        part_two = factor * (diagonal - centre) * current - (sigma * sigma_next) * previous
        following = part_two - (factor * KINETIC) * near(j - 1, stacked)
        previous, current, sigma = current, following, sigma_next
    filt_ref[...] = current
    stacked = jnp.concatenate(split(current), axis=0)
    send_halo(DEGREE, stacked)

    if not gram:
        out_ref[...] = diagonal * current - KINETIC * near(DEGREE, stacked)
        for step in range(DEGREE + 1):
            done_halo(step)
        return

    app, fall, aall, give, keep, core_in, y_in, band_out, band_in = scratch[12:21]
    f_ss, f_rs, a_ss, a_rs, c_ss, c_rs, y_ss, y_rs, b_ss, b_rs = scratch[21:]
    wide = N // B

    def spread(src, dst, ss, rs):
        copies = []
        for o in range(1, B):
            to = lax.rem(b + o, B)
            copy = remote(
                src.at[:, pl.ds(pl.multiple_of(to * wide, wide), wide)],
                dst.at[b],
                ss.at[o - 1],
                rs.at[o - 1],
                {"band": to},
            )
            copy.start()
            copies.append(copy)
        dst[b] = src[:, pl.ds(pl.multiple_of(b * wide, wide), wide)]
        return copies

    f_copies = spread(filt_ref, fall, f_ss, f_rs)
    app[...] = diagonal * current - KINETIC * near(DEGREE, stacked)
    a_copies = spread(app, aall, a_ss, a_rs)
    for copy in f_copies:
        copy.wait_recv()
    orbs = B * R
    left = fall[...].reshape(orbs, wide)
    left_hi, left_lo = split(left)
    left_both = jnp.concatenate([left_hi, left_lo], axis=0)
    for copy in a_copies:
        copy.wait_recv()

    blocks = B // D
    core = lax.rem(d, 2)
    pair = d // 2
    rights = (((1,), (1,)), ((), ()))

    def partial(target):
        start = target * blocks
        right = jnp.concatenate(
            [
                fall[pl.ds(start, blocks)].reshape(blocks * R, wide),
                aall[pl.ds(start, blocks)].reshape(blocks * R, wide),
            ],
            axis=0,
        )
        right_hi, right_lo = split(right)
        both = lax.dot_general(left_both, right_hi, rights, preferred_element_type=f32)
        low = lax.dot_general(left_hi, right_lo, rights, preferred_element_type=f32)
        return both[:orbs] + both[orbs:] + low

    pairs = D // 2
    chunks = D
    per = B // chunks
    height = per * R
    order = [lax.rem(b // per + 1 + i, chunks) for i in range(chunks)]
    spans = [pl.ds(pl.multiple_of(h * height, height), height) for h in order]
    c_copies = []
    for q in range(pairs):
        turn = lax.rem(pair + 1 + q, pairs)
        give[q] = partial(2 * turn + (1 - core))
        row = []
        for i in range(chunks):
            copy = remote(
                give.at[q, spans[i]],
                core_in.at[q, spans[i]],
                c_ss.at[q, i],
                c_rs.at[q, i],
                {"domain": 2 * pair + 1 - core},
            )
            copy.start()
            row.append(copy)
        c_copies.append(row)
    for q in range(pairs):
        keep[q] = partial(2 * lax.rem(pair + 1 + q, pairs) + core)
    y_copies = []
    for q in range(pairs - 1):
        turn = lax.rem(pair + 1 + q, pairs)
        row = []
        for i in range(chunks):
            c_copies[q][i].wait_recv()
            keep[q, spans[i]] = keep[q, spans[i]] + core_in[q, spans[i]]
            copy = remote(
                keep.at[q, spans[i]],
                y_in.at[q, spans[i]],
                y_ss.at[q, i],
                y_rs.at[q, i],
                {"domain": 2 * turn + core},
            )
            copy.start()
            row.append(copy)
        y_copies.append(row)

    def band_copy(to):
        return remote(band_out.at[to], band_in.at[b], b_ss.at[to], b_rs.at[b], {"band": to})

    for i in range(chunks):
        c_copies[pairs - 1][i].wait_recv()
        total = keep[pairs - 1, spans[i]] + core_in[pairs - 1, spans[i]]
        for q in range(pairs - 1):
            y_copies[q][i].wait_recv()
            total = total + y_in[q, spans[i]]
        total = total * (1.0 / (N * D))
        for t in range(per):
            to = order[i] * per + t
            band_out[to] = total[t * R : (t + 1) * R]
            pl.when(to != b)(band_copy(to).start)
    result = band_out[b]
    for o in range(1, B):
        other = lax.rem(b + o, B)
        remote(
            band_out.at[other], band_in.at[other], b_ss.at[other], b_rs.at[other], {"band": other}
        ).wait_recv()
        result = result + band_in[other]
    out_ref[...] = result
    for o in range(1, B):
        band_copy(lax.rem(b + o, B)).wait_send()
    for step in range(DEGREE + 1):
        done_halo(step)
    for copy in f_copies + a_copies + sum(c_copies + y_copies, []):
        copy.wait_send()


def inner_products(left_block, right_block):
    return lax.dot_general(
        left_block,
        right_block,
        (((1,), (1,)), ((), ())),
        precision=lax.Precision.HIGHEST,
        preferred_element_type=f32,
    )


def shards(orbitals, potential, stencil, send_list, send_count):
    D, B = lax.axis_size("domain"), lax.axis_size("band")
    R, N = orbitals.shape
    cap = send_list.shape[1]
    orbs = R * B
    keys = N + 2 * cap
    gram = D == 4 and N % (128 * B) == 0 and B % D == 0 and 2 * orbs // D == 128
    steps = DEGREE + 1
    dma = pltpu.SemaphoreType.DMA
    scratch = [
        pltpu.VMEM((R, N), f32),
        pltpu.VMEM((1, N), f32),
        pltpu.VMEM(stencil.shape, i32),
        pltpu.VMEM(send_list.shape, i32),
        dma((4,)),
        pltpu.VMEM((keys, N), bf16),
        pltpu.VMEM((keys, N), bf16),
        pltpu.VMEM((N, 2 * cap), bf16),
        pltpu.VMEM(stencil.shape, i32),
        pltpu.VMEM(stencil.shape, i32),
        pltpu.VMEM((D, 8, 128), f32),
        pltpu.VMEM((steps, 2, R, cap), f32),
        pltpu.VMEM((steps, 2, R, cap), f32),
        dma((D - 1,)),
        dma((D - 1,)),
        dma((steps, 2)),
        dma((steps, 2)),
    ]
    if gram:
        wide = N // B
        width = 2 * orbs // D
        pairs = D // 2
        scratch += [
            pltpu.VMEM((R, N), f32),
            pltpu.VMEM((B, R, wide), f32),
            pltpu.VMEM((B, R, wide), f32),
            pltpu.VMEM((pairs, orbs, width), f32),
            pltpu.VMEM((pairs, orbs, width), f32),
            pltpu.VMEM((pairs, orbs, width), f32),
            pltpu.VMEM((pairs - 1, orbs, width), f32),
            pltpu.VMEM((B, R, width), f32),
            pltpu.VMEM((B, R, width), f32),
        ]
        for counts in ((B - 1,), (B - 1,), (pairs, D), (pairs - 1, D), (B,)):
            scratch += [dma(counts), dma(counts)]
    second = (R, 2 * orbs // D) if gram else (R, N)
    filtered, other = pl.pallas_call(
        functools.partial(kernel, D, B, gram),
        out_shape=(
            jax.ShapeDtypeStruct((R, N), f32),
            jax.ShapeDtypeStruct(second, f32),
        ),
        in_specs=[pl.BlockSpec(memory_space=pltpu.HBM)] * 4
        + [pl.BlockSpec(memory_space=pltpu.VMEM)],
        out_specs=[pl.BlockSpec(memory_space=pltpu.VMEM)] * 2,
        scratch_shapes=scratch,
        compiler_params=pltpu.CompilerParams(
            collective_id=0, has_side_effects=True, vmem_limit_bytes=48 * 1024 * 1024
        ),
    )(orbitals, potential.reshape(1, N), stencil, send_list, send_count)
    if gram:
        half = orbs // D
        return filtered, other[:, :half], other[:, half:]
    results = []
    for block in (filtered, other):
        whole = lax.all_gather(block, "band", axis=0, tiled=True)
        share = inner_products(filtered, whole)
        total = lax.psum_scatter(share, "domain", scatter_dimension=1, tiled=True)
        results.append(total / (N * D))
    return filtered, results[0], results[1]


def solution(mesh):
    placed = (
        P("band", "domain"),
        P("domain"),
        P(None, "domain"),
        P(None, "domain"),
        P(None, "domain"),
    )
    return jax.shard_map(
        shards,
        mesh=mesh,
        in_specs=placed,
        out_specs=(P("band", "domain"), P("band", "domain"), P("band", "domain")),
        check_vma=False,
    )
```
